32 devices in a mesh: clip: 2 (over x), gx: 8 (over z, y), gy: 2 (over core).
Axes of the slice: x: 2, y: 2, z: 4, core: 2. Of those that a mesh axis runs over, the one named last changes fastest.
Arguments:
- e_field: float32 [3, 128, 128, 128], P(None, ('clip', 'gx'), 'gy'), parts along dimension 1, may hold values from -6 to 6
- h_field: float32 [3, 128, 128, 128], P(None, ('clip', 'gx'), 'gy'), parts along dimension 1, may hold values from -6 to 6
- material: int32 [128, 128, 128], P(('clip', 'gx'), 'gy'), parts along dimension 0, may hold values from 0 to 5
- eps_table: float32 [6], replicated, may hold values from 0.8 to 1.2
- sigma_table: float32 [6], replicated, may hold values from 0 to 2
- angle_orders: int32 [64, 2], replicated, may hold values from -8 to 8
Outputs:
- e_out: float32 [3, 128, 128, 128], P(None, ('clip', 'gx'), 'gy'), parts along dimension 1
- h_out: float32 [3, 128, 128, 128], P(None, ('clip', 'gx'), 'gy'), parts along dimension 1
- far_field: float32 [128, 4], P(('clip', 'gx')), parts along dimension 0
The draws below stay inside these ranges and needn't reach their ends.
There are 2 independent parts, one for each index of `clip`. The reference program is written for one: setup_inputs(seed, part) draws one part's arguments, and reference() takes and returns one part's arrays. A program takes and returns all parts, laid end to end along the dimension named above; an argument that names none is the same for every part. Nothing has to cross between parts.
All inputs are finite; a program needn't handle non-finite values.
Results may differ from the reference program's by a relative error of at most 0.00021.
Values sent between devices are 32-bit elements; how exact they have to be, the bound alone decides.
A program may use at most 64 MiB of HBM per device.

```python
import math
import jax
import jax.numpy as jnp
from jax import lax

NZ = 128
BILAYERS = 18
MATS = 6
ANGLES = 64
ITERS = 4
NX = 64
NY = 128


def draw_material(key, part):
    key_pattern = jax.random.fold_in(key, 11)
    key_mixing = jax.random.fold_in(key, 12)
    key_random = jax.random.fold_in(key, 13)
    depth = jnp.arange(NZ, dtype=jnp.int32)
    period = depth % 6
    stack_ids = jnp.where(period < 2, 1, jnp.where(period == 2, 4, 2))
    summit = 6 * BILAYERS
    column = jnp.where(depth < summit, stack_ids, jnp.where(depth < summit + 2, 3, jnp.where(depth < summit + 10, 5, 0)))
    pattern = jax.random.randint(key_pattern, (NX, NY), 0, 2)
    pattern = pattern.at[0].set(1)
    absorber_band = (depth >= summit + 2) & (depth < summit + 10)
    layered = jnp.where(absorber_band[None, None, :] & (pattern[:, :, None] == 0), 0, column[None, None, :])
    mixing = jax.random.randint(key_mixing, (NX, NY, NZ), 0, 4)
    random_ids = jax.random.randint(key_random, (NX, NY, NZ), 0, MATS)
    return jnp.where(mixing == 0, random_ids, layered).astype(jnp.int32)


def place_ends(result, key, smallest, high):
    longest = result.shape.index(max(result.shape))
    spots = []
    for shift in (0, 1):
        where = [jax.random.randint(jax.random.fold_in(key, axis), (), 0, length) for axis, length in enumerate(result.shape)]
        where[longest] = (where[longest] + shift) % result.shape[longest]
        spots.append(tuple(where))
    return result.at[spots[0]].set(smallest).at[spots[1]].set(high)


def levels(key, shape, cuts, low, high):
    level = 1.0
    for axis_at, blocks in cuts:
        steps = jax.random.uniform(jax.random.fold_in(jax.random.fold_in(key, 6), axis_at), (blocks,), jnp.float32, low / len(cuts), high / len(cuts))
        level = level * jnp.repeat(jnp.exp(steps), shape[axis_at] // blocks).reshape((-1,) + (1,) * (len(shape) - 1 - axis_at))
    return level


def noise(stream_key, extent, spread, limit, shards=(), kind=jnp.bfloat16):
    factor_of = levels(stream_key, extent, shards, -0.22, 0.18) if shards else 1.0
    values = jax.random.normal(stream_key, extent, jnp.float32) * spread * factor_of
    return jnp.minimum(jnp.maximum(values, -limit), limit).astype(kind)


def setup_inputs(seed: int = 0, part: int = 0) -> dict:
    key_of = jax.random.split(jax.random.key(seed), 7)
    part_keys = jax.random.split(jax.random.fold_in(key_of[6], part), 7)
    return {
        "e_field": noise(part_keys[0], (3, NX, NY, NZ), 1.0, 6.0, ((1, 8), (2, 2)), jnp.float32),
        "h_field": noise(part_keys[1], (3, NX, NY, NZ), 1.0, 6.0, ((1, 8), (2, 2)), jnp.float32),
        "material": draw_material(jax.random.fold_in(jax.random.fold_in(key_of[6], part), 71), part),
        "eps_table": jnp.clip(jax.random.uniform(key_of[3], (MATS,), jnp.float32, 0.8, 1.2), 0.8, 1.2),
        "sigma_table": jnp.clip(jax.random.uniform(key_of[4], (MATS,), jnp.float32, 0.0, 2.0), 0.0, 2.0),
        "angle_orders": place_ends(jax.random.randint(key_of[5], (ANGLES, 2), -8, 9), jax.random.fold_in(key_of[5], 1), -8, 8).astype(jnp.int32),
    }


TIME_STEP = 0.5
PHASE_STEP = 0.9

def forward(field, axis):
    if axis == 2:
        upper = jnp.concatenate([field[..., 1:], jnp.zeros_like(field[..., :1])], axis=-1)
    else:
        upper = jnp.roll(field, -1, axis)
    return upper - field

def backward(field, axis):
    if axis == 2:
        lower = jnp.concatenate([jnp.zeros_like(field[..., :1]), field[..., :-1]], axis=-1)
    else:
        lower = jnp.roll(field, 1, axis)
    return field - lower

def reference(e_field, h_field, material, eps_table, sigma_table, angle_orders):
    permit = eps_table[material]
    conduct = sigma_table[material]
    loss = conduct * TIME_STEP / (2.0 * permit)
    keep = (1.0 - loss) / (1.0 + loss)
    drive = TIME_STEP / (permit * (1.0 + loss))
    elec_x, elec_y, elec_z = (e_field[0], e_field[1], e_field[2])
    magn_x, magn_y, magn_z = (h_field[0], h_field[1], h_field[2])
    mon_real = jnp.zeros((2, NX, NY), jnp.float32)
    mon_imag = jnp.zeros((2, NX, NY), jnp.float32)
    for number in range(ITERS):
        magn_x = magn_x - TIME_STEP * (forward(elec_z, 1) - forward(elec_y, 2))
        magn_y = magn_y - TIME_STEP * (forward(elec_x, 2) - forward(elec_z, 0))
        magn_z = magn_z - TIME_STEP * (forward(elec_y, 0) - forward(elec_x, 1))
        elec_x = keep * elec_x + drive * (backward(magn_z, 1) - backward(magn_y, 2))
        elec_y = keep * elec_y + drive * (backward(magn_x, 2) - backward(magn_z, 0))
        elec_z = keep * elec_z + drive * (backward(magn_y, 0) - backward(magn_x, 1))
        plane = jnp.stack([elec_x[:, :, NZ - 3], elec_y[:, :, NZ - 3]])
        mon_real = mon_real + math.cos(PHASE_STEP * (number + 1)) * plane
        mon_imag = mon_imag - math.sin(PHASE_STEP * (number + 1)) * plane
    pos_x = jnp.arange(NX, dtype=jnp.int32)
    pos_y = jnp.arange(NY, dtype=jnp.int32)
    order_x = angle_orders[:, 0].astype(jnp.int32)
    order_y = angle_orders[:, 1].astype(jnp.int32)
    phase_int = (order_x[:, None, None] * pos_x[None, :, None] * NY + order_y[:, None, None] * pos_y[None, None, :] * NX) % (NX * NY)
    theta = phase_int.astype(jnp.float32) * (2.0 * math.pi / (NX * NY))
    cosine = jnp.cos(theta).reshape(ANGLES, NX * NY)
    sine = jnp.sin(theta).reshape(ANGLES, NX * NY)
    flat_real = mon_real.reshape(2, NX * NY).T
    flat_imag = mon_imag.reshape(2, NX * NY).T
    high = lax.Precision.HIGHEST
    real_part = jnp.dot(cosine, flat_real, precision=high, preferred_element_type=jnp.float32) + jnp.dot(sine, flat_imag, precision=high, preferred_element_type=jnp.float32)
    imag_part = jnp.dot(cosine, flat_imag, precision=high, preferred_element_type=jnp.float32) - jnp.dot(sine, flat_real, precision=high, preferred_element_type=jnp.float32)
    far_field = jnp.stack([real_part[:, 0], imag_part[:, 0], real_part[:, 1], imag_part[:, 1]], axis=1) * (1.0 / math.sqrt(NX * NY))
    e_out = jnp.stack([elec_x, elec_y, elec_z])
    h_out = jnp.stack([magn_x, magn_y, magn_z])
    return (e_out, h_out, far_field)
```

```python
import functools
import math

import jax
import jax.numpy as jnp
from jax import lax
from jax.experimental import pallas as pl
from jax.experimental.pallas import tpu as pltpu
from jax.sharding import PartitionSpec as P

ITERS = 4
TIME_STEP = 0.5
PHASE_STEP = 0.9
MESH = pl.DeviceIdType.MESH
PAD = 8
HIGH = lax.Precision.HIGHEST

FWD, BACK, ROW_E, ROW_H, CORNER_E, CORNER_H = range(6)


def kernel(
    size_x, size_y,
    eps_ref, sigma_ref, orders_ref, e_in, h_in, mat_in,
    e_out, h_out, far_ref,
    elec, magn, mat, coef, mon, tables,
    fwd_send, fwd_recv, back_send, back_recv,
    rowe_send, rowe_recv, rowh_send, rowh_recv,
    core_send, core_recv, corh_send, corh_recv,
    terms_send, terms_recv,
    load_sem, store_sem, send_sem, recv_sem, far_send_sem, far_recv_sem,
):
    cells_x, cells_y, depth = mat.shape
    last = cells_x - 1
    chunk = min(32, cells_y)
    starts = range(0, cells_y, chunk)
    me_x = lax.axis_index("gx")
    me_y = lax.axis_index("gy")
    right = lax.rem(me_x + 1, size_x)
    left = lax.rem(me_x + size_x - 1, size_x)
    above = lax.rem(me_y + 1, size_y)
    below = lax.rem(me_y + size_y - 1, size_y)
    group = size_x * size_y
    me = me_x * size_y + me_y

    def load(src, dst, sem):
        copy = pltpu.make_async_copy(src, dst, load_sem.at[sem])
        copy.start()
        return copy

    inner = pl.ds(0, last)
    ebody = pl.ds(0, cells_y)
    hbody = pl.ds(PAD, cells_y)
    edge_e = load(e_in.at[:, last], elec.at[:, last, ebody], 0)
    edge_h = load(h_in.at[:, last], magn.at[:, last, hbody], 1)
    rest_e = load(e_in.at[:, inner], elec.at[:, inner, ebody], 2)
    rest_h = load(h_in.at[:, inner], magn.at[:, inner, hbody], 3)
    load_mat = load(mat_in, mat, 4)

    def member(offset):
        index = lax.rem(me + offset, group)
        return index // size_y, lax.rem(index, size_y)

    barrier = pltpu.get_barrier_semaphore()
    for offset in range(1, group):
        tx, ty = member(offset)
        pl.semaphore_signal(barrier, inc=1, device_id={"gx": tx, "gy": ty}, device_id_type=MESH)

    lane = lax.broadcasted_iota(jnp.int32, (chunk, depth), 1)
    first_lane = lane == 0
    last_lane = lane == depth - 1

    def forward_z(value):
        return jnp.where(last_lane, 0.0, pltpu.roll(value, depth - 1, 1)) - value

    def backward_z(value):
        return value - jnp.where(first_lane, 0.0, pltpu.roll(value, 1, 1))

    elec[:, :, pl.ds(cells_y, PAD), :] = jnp.zeros((3, cells_x, PAD, depth), jnp.float32)

    def copy_to(phase, kind, src, dst, tx, ty):
        return pltpu.make_async_remote_copy(
            src_ref=src, dst_ref=dst,
            send_sem=send_sem.at[phase, kind], recv_sem=recv_sem.at[phase, kind],
            device_id={"gx": tx, "gy": ty}, device_id_type=MESH,
        )

    def fwd_copy(k):
        return copy_to(k, FWD, fwd_send.at[k], fwd_recv.at[k], right, me_y)

    def back_copy(k):
        src = e_in.at[pl.ds(1, 2), 0] if k == 0 else back_send.at[k]
        return copy_to(k, BACK, src, back_recv.at[k], left, me_y)

    def rowe_copy(k):
        return copy_to(k, ROW_E, rowe_send.at[k], rowe_recv.at[k], me_x, below)

    def rowh_copy(k):
        return copy_to(k, ROW_H, rowh_send.at[k], rowh_recv.at[k], me_x, above)

    def core_copy(k):
        return copy_to(k, CORNER_E, core_send.at[k], core_recv.at[k], right, below)

    def corh_copy(k):
        return copy_to(k, CORNER_H, corh_send.at[k], corh_recv.at[k], left, above)

    def magn_plane(x, ahead, stage=None):
        for r in starts:
            rows, upper, hrows = pl.ds(r, chunk), pl.ds(r + 1, chunk), pl.ds(PAD + r, chunk)
            ex, ey, ez = elec[0, x, rows], elec[1, x, rows], elec[2, x, rows]
            dyx = elec[0, x, upper] - ex
            dyz = elec[2, x, upper] - ez
            if ahead is None:
                dxy, dxz = -ey, -ez
            else:
                dxy, dxz = elec[1, ahead, rows] - ey, elec[2, ahead, rows] - ez
            hy = magn[1, x, hrows] - TIME_STEP * (forward_z(ex) - dxz)
            hz = magn[2, x, hrows] - TIME_STEP * (dxy - dyx)
            magn[0, x, hrows] = magn[0, x, hrows] - TIME_STEP * (dyz - forward_z(ey))
            magn[1, x, hrows] = hy
            magn[2, x, hrows] = hz
            if stage is not None:
                fwd_send[stage, 0, rows] = hy
                fwd_send[stage, 1, rows] = hz

    def elec_plane(x, previous, number, stage=None):
        cos_n = math.cos(PHASE_STEP * number)
        sin_n = math.sin(PHASE_STEP * number)
        for r in starts:
            rows, hrows, lower = pl.ds(r, chunk), pl.ds(PAD + r, chunk), pl.ds(PAD + r - 1, chunk)
            hx, hy, hz = magn[0, x, hrows], magn[1, x, hrows], magn[2, x, hrows]
            ex, ey, ez = elec[0, x, rows], elec[1, x, rows], elec[2, x, rows]
            prev_y, prev_z = previous(r, ey, ez)
            keep, drive = coef[0, x, rows], coef[1, x, rows]
            new_x = keep * ex + drive * ((hz - magn[2, x, lower]) - backward_z(hy))
            new_y = keep * ey + drive * (backward_z(hx) - (hz - prev_z))
            new_z = keep * ez + drive * ((hy - prev_y) - (hx - magn[0, x, lower]))
            elec[0, x, rows] = new_x
            elec[1, x, rows] = new_y
            elec[2, x, rows] = new_z
            if stage is not None:
                back_send[stage, 0, rows] = new_y
                back_send[stage, 1, rows] = new_z
            total = mon[rows]
            for comp, new in ((0, new_x), (1, new_y)):
                slot = comp * cells_x + x
                weight = jnp.where(lane == slot, cos_n, jnp.where(lane == slot + 2 * cells_x, -sin_n, 0.0))
                total = total + jnp.broadcast_to(new[:, depth - 3:depth - 2], (chunk, depth)) * weight
            mon[rows] = total

    def local_previous(x):
        def previous(r, ey, ez):
            hrows = pl.ds(PAD + r, chunk)
            return magn[1, x - 1, hrows], magn[2, x - 1, hrows]
        return previous

    def send_back(k):
        if k == 0:
            corh_send[k] = elec[1, 0, pl.ds(cells_y - 8, 8)]
        else:
            corh_send[k] = back_send[k, 0, pl.ds(cells_y - 8, 8)]
            back_copy(k).start()
        corh_copy(k).start()

    def send_fwd(k):
        core_send[k] = elec[0, last, pl.ds(0, 8)]
        fwd_copy(k).start()
        core_copy(k).start()

    mon[...] = jnp.zeros_like(mon)
    edge_e.wait()
    edge_h.wait()
    magn_plane(last, None, 0)
    pl.semaphore_wait(barrier, group - 1)
    back_copy(0).start()
    send_fwd(0)
    rest_e.wait()
    send_back(0)
    rest_h.wait()

    row63 = pl.ds(PAD + cells_y - 1, 1)
    halo = pl.ds(PAD - 1, 1)
    row0 = pl.ds(0, 1)

    stores = []

    def store(src, dst):
        copy = pltpu.make_async_copy(src, dst, store_sem.at[len(stores)])
        copy.start()
        stores.append(copy)

    for k in range(ITERS):
        def magn_body(x, carry):
            magn_plane(x, x + 1)
            return carry

        lax.fori_loop(0, last, magn_body, 0)
        rowe_send[k, 0] = elec[0, :, row0]
        rowe_send[k, 1] = elec[2, :, row0]
        rowh_send[k, 0] = magn[0, :, row63]
        rowh_send[k, 1] = magn[2, :, row63]
        rowe_copy(k).start()
        rowh_copy(k).start()
        if k == 0:
            load_mat.wait()
            count = eps_ref.shape[0]
            keeps, drives = [], []
            for m in range(count):
                permit = jnp.full((8, depth), eps_ref[m], jnp.float32)
                conduct = jnp.full((8, depth), sigma_ref[m], jnp.float32)
                loss = conduct * TIME_STEP / (2.0 * permit)
                keeps.append(((1.0 - loss) / (1.0 + loss))[:1])
                drives.append((TIME_STEP / (permit * (1.0 + loss)))[:1])

            def coef_body(x, carry):
                for r in starts:
                    rows = pl.ds(r, chunk)
                    ids = mat[x, rows]
                    keep = jnp.broadcast_to(keeps[0], (chunk, depth))
                    drive = jnp.broadcast_to(drives[0], (chunk, depth))
                    for m in range(1, count):
                        keep = jnp.where(ids == m, keeps[m], keep)
                        drive = jnp.where(ids == m, drives[m], drive)
                    coef[0, x, rows] = keep
                    coef[1, x, rows] = drive
                return carry

            lax.fori_loop(0, cells_x, coef_body, 0)
        if k == 1:
            shape = (orders_ref.shape[0], depth)
            wide = lax.broadcasted_iota(jnp.int32, shape, 1)
            for slot, axis, pos, extent in (
                (0, 1, me_y * cells_y + wide, size_y * cells_y),
                (2, 0, me_x * cells_x + lax.rem(wide, cells_x), size_x * cells_x),
            ):
                order = jnp.broadcast_to(orders_ref[:, axis:axis + 1], shape)
                turns = (order * pos).astype(jnp.float32) * (1.0 / extent)
                angle = (turns - jnp.floor(turns)) * (2.0 * math.pi)
                tables[slot] = jnp.cos(angle)
                tables[slot + 1] = jnp.sin(angle)

        rowe_copy(k).wait_recv()
        rowh_copy(k).wait_recv()
        magn[0, :, row63] = magn[0, :, row63] - TIME_STEP * rowe_recv[k, 1]
        magn[2, :, row63] = magn[2, :, row63] + TIME_STEP * rowe_recv[k, 0]
        magn[0, :, halo] = rowh_recv[k, 0] - TIME_STEP * elec[2, :, row0]
        magn[2, :, halo] = rowh_recv[k, 1] + TIME_STEP * elec[0, :, row0]

        def elec_body(x, carry):
            elec_plane(x, local_previous(x), k + 1)
            return carry

        lax.fori_loop(1, last, elec_body, 0)
        final = k == ITERS - 1
        if final:
            store(magn.at[:, inner, hbody], h_out.at[:, inner])
            store(elec.at[:, pl.ds(1, last - 1), ebody], e_out.at[:, pl.ds(1, last - 1)])

        fwd_copy(k).wait_recv()
        core_copy(k).wait_recv()
        fwd_recv[k, 1, pl.ds(cells_y - 1, 1)] = (
            fwd_recv[k, 1, pl.ds(cells_y - 1, 1)] + TIME_STEP * core_recv[k, pl.ds(0, 1)]
        )

        def received(r, ey, ez):
            rows = pl.ds(r, chunk)
            return fwd_recv[k, 0, rows] + TIME_STEP * ez, fwd_recv[k, 1, rows] - TIME_STEP * ey

        elec_plane(0, received, k + 1, None if final else k + 1)
        if not final:
            send_back(k + 1)
        else:
            store(elec.at[:, 0, ebody], e_out.at[:, 0])

        back_copy(k).wait_recv()
        corh_copy(k).wait_recv()
        for r in starts:
            rows, hrows = pl.ds(r, chunk), pl.ds(PAD + r, chunk)
            magn[1, last, hrows] = magn[1, last, hrows] + TIME_STEP * back_recv[k, 1, rows]
            magn[2, last, hrows] = magn[2, last, hrows] - TIME_STEP * back_recv[k, 0, rows]
        magn[2, last, halo] = magn[2, last, halo] - TIME_STEP * corh_recv[k, pl.ds(7, 1)]
        elec_plane(last, local_previous(last), k + 1)
        if not final:
            magn_plane(last, None, k + 1)
            send_fwd(k + 1)
        else:
            store(magn.at[:, last, hbody], h_out.at[:, last])
            store(elec.at[:, last, ebody], e_out.at[:, last])

    span = 2 * cells_x
    total = mon[...]
    by_cos = jnp.dot(tables[0, :, pl.ds(0, cells_y)], total, precision=HIGH, preferred_element_type=jnp.float32)
    by_sin = jnp.dot(tables[1, :, pl.ds(0, cells_y)], total, precision=HIGH, preferred_element_type=jnp.float32)
    part_re = by_cos + pltpu.roll(by_sin, depth - span, 1)
    part_im = pltpu.roll(by_cos, depth - span, 1) - by_sin
    cos_x, sin_x = tables[2], tables[3]
    wide = lax.broadcasted_iota(jnp.int32, part_re.shape, 1)
    real = jnp.where(wide < span, cos_x * part_re + sin_x * part_im, 0.0)
    imag = jnp.where(wide < span, cos_x * part_im - sin_x * part_re, 0.0)
    both = real + pltpu.roll(imag, span, 1)
    owned = terms_send.shape[1]
    for peer in range(size_x):
        terms_send[peer] = both[peer * owned:(peer + 1) * owned]

    def far_copy(offset):
        tx, ty = member(offset)
        return pltpu.make_async_remote_copy(
            src_ref=terms_send.at[tx], dst_ref=terms_recv.at[me],
            send_sem=far_send_sem.at[offset], recv_sem=far_recv_sem.at[me],
            device_id={"gx": tx, "gy": ty}, device_id_type=MESH,
        )

    for offset in range(1, group):
        far_copy(offset).start()
    answer = terms_send[me_x]
    for offset in range(1, group):
        source = lax.rem(me + offset, group)
        pltpu.make_async_remote_copy(
            src_ref=terms_send.at[0], dst_ref=terms_recv.at[source],
            send_sem=far_send_sem.at[offset], recv_sem=far_recv_sem.at[source],
            device_id={"gx": right, "gy": me_y}, device_id_type=MESH,
        ).wait_recv()
        answer = answer + terms_recv[source]
    source_lane = lax.broadcasted_iota(jnp.int32, (depth, depth), 0) // cells_x
    target_lane = lax.broadcasted_iota(jnp.int32, (depth, depth), 1)
    picked = jnp.where(source_lane < 2, 2 * source_lane, 2 * source_lane - 3)
    pick = jnp.where((source_lane < 4) & (picked == target_lane), 1.0, 0.0)
    summed = jnp.dot(answer, pick, precision=HIGH, preferred_element_type=jnp.float32)
    scale = 1.0 / math.sqrt(size_x * cells_x * size_y * cells_y)
    far_ref[...] = summed[:, :4] * scale

    for copy in stores:
        copy.wait()
    for k in range(ITERS):
        for copy in (fwd_copy, back_copy, rowe_copy, rowh_copy, core_copy, corh_copy):
            copy(k).wait_send()
    for offset in range(1, group):
        far_copy(offset).wait_send()


def local(size_x, size_y, e_field, h_field, material, eps_table, sigma_table, angle_orders):
    cells_x, cells_y, depth = material.shape
    angles = angle_orders.shape[0]
    owned = angles // size_x
    group = size_x * size_y
    f32 = jnp.float32
    vmem = functools.partial(pl.BlockSpec, memory_space=pltpu.VMEM)
    smem = functools.partial(pl.BlockSpec, memory_space=pltpu.SMEM)
    hbm = functools.partial(pl.BlockSpec, memory_space=pl.ANY)
    dma = pltpu.SemaphoreType.DMA
    planes = pltpu.VMEM((ITERS, 2, cells_y, depth), f32)
    rows = pltpu.VMEM((ITERS, 2, cells_x, 1, depth), f32)
    corner = pltpu.VMEM((ITERS, 8, depth), f32)
    return pl.pallas_call(
        functools.partial(kernel, size_x, size_y),
        out_shape=(
            jax.ShapeDtypeStruct(e_field.shape, f32),
            jax.ShapeDtypeStruct(h_field.shape, f32),
            jax.ShapeDtypeStruct((owned, 4), f32),
        ),
        in_specs=[smem(), smem(), vmem(), hbm(), hbm(), hbm()],
        out_specs=(hbm(), hbm(), vmem()),
        scratch_shapes=[
            pltpu.VMEM((3, cells_x, cells_y + PAD, depth), f32),
            pltpu.VMEM((3, cells_x, cells_y + PAD, depth), f32),
            pltpu.VMEM((cells_x, cells_y, depth), jnp.int32),
            pltpu.VMEM((2, cells_x, cells_y, depth), f32),
            pltpu.VMEM((cells_y, depth), f32),
            pltpu.VMEM((4, angles, depth), f32),
            planes, planes, planes, planes,
            rows, rows, rows, rows,
            corner, corner, corner, corner,
            pltpu.VMEM((size_x, owned, depth), f32),
            pltpu.VMEM((group, owned, depth), f32),
            dma((5,)), dma((5,)), dma((ITERS, 6)), dma((ITERS, 6)), dma((group,)), dma((group,)),
        ],
        compiler_params=pltpu.CompilerParams(
            collective_id=0, has_side_effects=True, vmem_limit_bytes=32 * 1024 * 1024
        ),
    )(eps_table, sigma_table, angle_orders, e_field, h_field, material)


def solution(mesh):
    return jax.shard_map(
        functools.partial(local, mesh.shape["gx"], mesh.shape["gy"]),
        mesh=mesh,
        in_specs=(
            P(None, ("clip", "gx"), "gy", None),
            P(None, ("clip", "gx"), "gy", None),
            P(("clip", "gx"), "gy", None),
            P(),
            P(),
            P(),
        ),
        out_specs=(
            P(None, ("clip", "gx"), "gy", None),
            P(None, ("clip", "gx"), "gy", None),
            P(("clip", "gx"), None),
        ),
        check_vma=False,
    )
```

```python
import functools
import math

import jax
import jax.numpy as jnp
from jax import lax
from jax.experimental import pallas as pl
from jax.experimental.pallas import tpu as pltpu
from jax.sharding import PartitionSpec as P

ITERS = 4
TIME_STEP = 0.5
PHASE_STEP = 0.9
MESH = pl.DeviceIdType.MESH
PAD = 8
HIGH = lax.Precision.HIGHEST

FWD, BACK, ROW_E, ROW_H, CORNER_E, CORNER_H = range(6)


def kernel(
    size_x, size_y,
    eps_ref, sigma_ref, orders_ref, e_in, h_in, mat_in,
    e_out, h_out, far_ref,
    elec, magn, mat, coef, mon, table_y, table_x,
    fwd_send, fwd_recv, back_send, back_recv,
    rowe_send, rowe_recv, rowh_send, rowh_recv,
    core_send, core_recv, corh_send, corh_recv,
    terms_send, terms_recv,
    load_sem, store_sem, send_sem, recv_sem, far_send_sem, far_recv_sem,
):
    cells_x, cells_y, depth = mat.shape
    last = cells_x - 1
    chunk = min(32, cells_y)
    starts = range(0, cells_y, chunk)
    me_x = lax.axis_index("gx")
    me_y = lax.axis_index("gy")
    right = lax.rem(me_x + 1, size_x)
    left = lax.rem(me_x + size_x - 1, size_x)
    above = lax.rem(me_y + 1, size_y)
    below = lax.rem(me_y + size_y - 1, size_y)
    group = size_x * size_y
    me = me_x * size_y + me_y

    def load(src, dst, sem):
        copy = pltpu.make_async_copy(src, dst, load_sem.at[sem])
        copy.start()
        return copy

    inner = pl.ds(0, last)
    ebody = pl.ds(0, cells_y)
    hbody = pl.ds(PAD, cells_y)
    edge_e = load(e_in.at[:, last], elec.at[:, last, ebody], 0)
    edge_h = load(h_in.at[:, last], magn.at[:, last, hbody], 1)
    rest_e = [load(e_in.at[c, inner], elec.at[c, inner, ebody], 2 + c) for c in range(3)]
    rest_h = [load(h_in.at[c, inner], magn.at[c, inner, hbody], 5 + c) for c in range(3)]
    load_mat = load(mat_in, mat, 8)

    def member(offset):
        index = lax.rem(me + offset, group)
        return index // size_y, lax.rem(index, size_y)

    barrier = pltpu.get_barrier_semaphore()
    for offset in range(1, group):
        tx, ty = member(offset)
        pl.semaphore_signal(barrier, inc=1, device_id={"gx": tx, "gy": ty}, device_id_type=MESH)

    lane = lax.broadcasted_iota(jnp.int32, (chunk, depth), 1)
    first_lane = lane == 0
    last_lane = lane == depth - 1

    def forward_z(value):
        return jnp.where(last_lane, 0.0, pltpu.roll(value, depth - 1, 1)) - value

    def backward_z(value):
        return value - jnp.where(first_lane, 0.0, pltpu.roll(value, 1, 1))

    elec[:, :, pl.ds(cells_y, PAD), :] = jnp.zeros((3, cells_x, PAD, depth), jnp.float32)

    def copy_to(phase, kind, src, dst, tx, ty):
        return pltpu.make_async_remote_copy(
            src_ref=src, dst_ref=dst,
            send_sem=send_sem.at[phase, kind], recv_sem=recv_sem.at[phase, kind],
            device_id={"gx": tx, "gy": ty}, device_id_type=MESH,
        )

    def fwd_copy(k):
        return copy_to(k, FWD, fwd_send.at[k], fwd_recv.at[k], right, me_y)

    def back_copy(k):
        src = e_in.at[pl.ds(1, 2), 0] if k == 0 else back_send.at[k]
        return copy_to(k, BACK, src, back_recv.at[k], left, me_y)

    def rowe_copy(k):
        return copy_to(k, ROW_E, rowe_send.at[k], rowe_recv.at[k], me_x, below)

    def rowh_copy(k):
        return copy_to(k, ROW_H, rowh_send.at[k], rowh_recv.at[k], me_x, above)

    def core_copy(k):
        return copy_to(k, CORNER_E, core_send.at[k], core_recv.at[k], right, below)

    def corh_copy(k):
        return copy_to(k, CORNER_H, corh_send.at[k], corh_recv.at[k], left, above)

    def magn_plane(x, ahead, stage=None, parts=starts):
        for r in parts:
            rows, upper, hrows = pl.ds(r, chunk), pl.ds(r + 1, chunk), pl.ds(PAD + r, chunk)
            ex, ey, ez = elec[0, x, rows], elec[1, x, rows], elec[2, x, rows]
            dyx = elec[0, x, upper] - ex
            dyz = elec[2, x, upper] - ez
            if ahead is None:
                dxy, dxz = -ey, -ez
            else:
                dxy, dxz = elec[1, ahead, rows] - ey, elec[2, ahead, rows] - ez
            hy = magn[1, x, hrows] - TIME_STEP * (forward_z(ex) - dxz)
            hz = magn[2, x, hrows] - TIME_STEP * (dxy - dyx)
            magn[0, x, hrows] = magn[0, x, hrows] - TIME_STEP * (dyz - forward_z(ey))
            magn[1, x, hrows] = hy
            magn[2, x, hrows] = hz
            if stage is not None:
                fwd_send[stage, 0, rows] = hy
                fwd_send[stage, 1, rows] = hz

    def elec_plane(x, previous, number, stage=None):
        cos_n = math.cos(PHASE_STEP * number)
        sin_n = math.sin(PHASE_STEP * number)
        for r in starts:
            rows, hrows, lower = pl.ds(r, chunk), pl.ds(PAD + r, chunk), pl.ds(PAD + r - 1, chunk)
            hx, hy, hz = magn[0, x, hrows], magn[1, x, hrows], magn[2, x, hrows]
            ex, ey, ez = elec[0, x, rows], elec[1, x, rows], elec[2, x, rows]
            prev_y, prev_z = previous(r, ey, ez)
            keep, drive = coef[0, x, rows], coef[1, x, rows]
            new_x = keep * ex + drive * ((hz - magn[2, x, lower]) - backward_z(hy))
            new_y = keep * ey + drive * (backward_z(hx) - (hz - prev_z))
            new_z = keep * ez + drive * ((hy - prev_y) - (hx - magn[0, x, lower]))
            elec[0, x, rows] = new_x
            elec[1, x, rows] = new_y
            elec[2, x, rows] = new_z
            if stage is not None:
                back_send[stage, 0, rows] = new_y
                back_send[stage, 1, rows] = new_z
            total = mon[rows]
            for comp, new in ((0, new_x), (1, new_y)):
                slot = comp * cells_x + x
                weight = jnp.where(lane == slot, cos_n, jnp.where(lane == slot + 2 * cells_x, -sin_n, 0.0))
                total = total + jnp.broadcast_to(new[:, depth - 3:depth - 2], (chunk, depth)) * weight
            mon[rows] = total

    def local_previous(x):
        def previous(r, ey, ez):
            hrows = pl.ds(PAD + r, chunk)
            return magn[1, x - 1, hrows], magn[2, x - 1, hrows]
        return previous

    def send_back(k):
        if k == 0:
            corh_send[k] = elec[1, 0, pl.ds(cells_y - 8, 8)]
        else:
            corh_send[k] = back_send[k, 0, pl.ds(cells_y - 8, 8)]
            back_copy(k).start()
        corh_copy(k).start()

    def send_fwd(k):
        core_send[k] = elec[0, last, pl.ds(0, 8)]
        fwd_copy(k).start()
        core_copy(k).start()

    mon[...] = jnp.zeros_like(mon)
    terms_send[...] = jnp.zeros_like(terms_send)
    edge_e.wait()
    edge_h.wait()
    magn_plane(last, None, 0)
    pl.semaphore_wait(barrier, group - 1)
    back_copy(0).start()
    send_fwd(0)
    for copy in rest_e:
        copy.wait()
    send_back(0)
    for copy in rest_h:
        copy.wait()

    row63 = pl.ds(PAD + cells_y - 1, 1)
    halo = pl.ds(PAD - 1, 1)
    row0 = pl.ds(0, 1)

    stores = []

    def store(src, dst):
        copy = pltpu.make_async_copy(src, dst, store_sem.at[len(stores)])
        copy.start()
        stores.append(copy)

    for k in range(ITERS):
        rowe_send[k, 0] = elec[0, :, row0]
        rowe_send[k, 1] = elec[2, :, row0]
        rowe_copy(k).start()
        for x in range(last):
            magn_plane(x, x + 1, parts=starts[-1:])
        rowh_send[k, 0] = magn[0, :, row63]
        rowh_send[k, 1] = magn[2, :, row63]
        rowh_copy(k).start()
        for x in range(last):
            magn_plane(x, x + 1, parts=starts[:-1])
        if k == 0:
            load_mat.wait()
            count = eps_ref.shape[0]
            keeps, drives = [], []
            for m in range(count):
                permit = jnp.full((8, depth), eps_ref[m], jnp.float32)
                conduct = jnp.full((8, depth), sigma_ref[m], jnp.float32)
                loss = conduct * TIME_STEP / (2.0 * permit)
                keeps.append(((1.0 - loss) / (1.0 + loss))[:1])
                drives.append((TIME_STEP / (permit * (1.0 + loss)))[:1])

            def coef_body(x, carry):
                for r in starts:
                    rows = pl.ds(r, chunk)
                    ids = mat[x, rows]
                    keep = jnp.broadcast_to(keeps[0], (chunk, depth))
                    drive = jnp.broadcast_to(drives[0], (chunk, depth))
                    for m in range(1, count):
                        keep = jnp.where(ids == m, keeps[m], keep)
                        drive = jnp.where(ids == m, drives[m], drive)
                    coef[0, x, rows] = keep
                    coef[1, x, rows] = drive
                return carry

            lax.fori_loop(0, cells_x, coef_body, 0)
        if k == 1:
            orders = jnp.concatenate([orders_ref[...], orders_ref[...]], axis=1)
            for table, axis, extent in ((table_y, 1, size_y * cells_y), (table_x, 0, size_x * cells_x)):
                shape = table.shape
                pos = lax.broadcasted_iota(jnp.int32, shape, 0)
                if axis == 1:
                    pos = me_y * cells_y + pos
                else:
                    pos = me_x * cells_x + lax.rem(pos, cells_x)
                turns = (jnp.broadcast_to(orders[axis:axis + 1], shape) * pos).astype(jnp.float32) * (1.0 / extent)
                angle = (turns - jnp.floor(turns)) * (2.0 * math.pi)
                wide = lax.broadcasted_iota(jnp.int32, shape, 1)
                table[...] = jnp.where(wide < shape[1] // 2, jnp.cos(angle), jnp.sin(angle))

        rowe_copy(k).wait_recv()
        rowh_copy(k).wait_recv()
        magn[0, :, row63] = magn[0, :, row63] - TIME_STEP * rowe_recv[k, 1]
        magn[2, :, row63] = magn[2, :, row63] + TIME_STEP * rowe_recv[k, 0]
        magn[0, :, halo] = rowh_recv[k, 0] - TIME_STEP * elec[2, :, row0]
        magn[2, :, halo] = rowh_recv[k, 1] + TIME_STEP * elec[0, :, row0]

        for x in range(1, last):
            elec_plane(x, local_previous(x), k + 1)
        final = k == ITERS - 1
        if final:
            store(magn.at[:, inner, hbody], h_out.at[:, inner])
            store(elec.at[:, pl.ds(1, last - 1), ebody], e_out.at[:, pl.ds(1, last - 1)])

        fwd_copy(k).wait_recv()
        core_copy(k).wait_recv()
        fwd_recv[k, 1, pl.ds(cells_y - 1, 1)] = (
            fwd_recv[k, 1, pl.ds(cells_y - 1, 1)] + TIME_STEP * core_recv[k, pl.ds(0, 1)]
        )

        def received(r, ey, ez):
            rows = pl.ds(r, chunk)
            return fwd_recv[k, 0, rows] + TIME_STEP * ez, fwd_recv[k, 1, rows] - TIME_STEP * ey

        elec_plane(0, received, k + 1, None if final else k + 1)
        if not final:
            send_back(k + 1)
        else:
            store(elec.at[:, 0, ebody], e_out.at[:, 0])

        back_copy(k).wait_recv()
        corh_copy(k).wait_recv()
        for r in starts:
            rows, hrows = pl.ds(r, chunk), pl.ds(PAD + r, chunk)
            magn[1, last, hrows] = magn[1, last, hrows] + TIME_STEP * back_recv[k, 1, rows]
            magn[2, last, hrows] = magn[2, last, hrows] - TIME_STEP * back_recv[k, 0, rows]
        magn[2, last, halo] = magn[2, last, halo] - TIME_STEP * corh_recv[k, pl.ds(7, 1)]
        elec_plane(last, local_previous(last), k + 1)
        if not final:
            magn_plane(last, None, k + 1)
            send_fwd(k + 1)
        else:
            store(magn.at[:, last, hbody], h_out.at[:, last])
            store(elec.at[:, last, ebody], e_out.at[:, last])

    span = 2 * cells_x
    total = jnp.transpose(mon[...])[:2 * span]
    by_cos = jnp.dot(total, table_y[...], precision=HIGH, preferred_element_type=jnp.float32)
    angles = by_cos.shape[1] // 2
    by_sin = pltpu.roll(by_cos, angles, 1)
    part_re = by_cos[:span] + by_sin[span:]
    part_im = by_cos[span:] - by_sin[:span]
    cos_x = table_x[...]
    sin_x = pltpu.roll(cos_x, angles, 1)
    real = cos_x * part_re + sin_x * part_im
    imag = cos_x * part_im - sin_x * part_re
    for row, value in enumerate((real[:cells_x], imag[:cells_x], real[cells_x:], imag[cells_x:])):
        terms_send[row:row + 1] = jnp.sum(value, axis=0, keepdims=True)

    def far_copy(offset):
        tx, ty = member(offset)
        return pltpu.make_async_remote_copy(
            src_ref=terms_send, dst_ref=terms_recv.at[me],
            send_sem=far_send_sem.at[offset], recv_sem=far_recv_sem.at[me],
            device_id={"gx": tx, "gy": ty}, device_id_type=MESH,
        )

    for offset in range(1, group):
        far_copy(offset).start()
    answer = terms_send[...]
    for offset in range(1, group):
        source = lax.rem(me + offset, group)
        pltpu.make_async_remote_copy(
            src_ref=terms_send, dst_ref=terms_recv.at[source],
            send_sem=far_send_sem.at[offset], recv_sem=far_recv_sem.at[source],
            device_id={"gx": right, "gy": me_y}, device_id_type=MESH,
        ).wait_recv()
        answer = answer + terms_recv[source]
    owned = far_ref.shape[1]
    width = answer.shape[1]
    mine = pltpu.roll(answer, lax.rem(width - owned * me_x, width), 1)
    scale = 1.0 / math.sqrt(size_x * cells_x * size_y * cells_y)
    far_ref[...] = mine[:4, :owned] * scale

    for copy in stores:
        copy.wait()
    for k in range(ITERS):
        for copy in (fwd_copy, back_copy, rowe_copy, rowh_copy, core_copy, corh_copy):
            copy(k).wait_send()
    for offset in range(1, group):
        far_copy(offset).wait_send()


def local(size_x, size_y, e_field, h_field, material, eps_table, sigma_table, angle_orders):
    cells_x, cells_y, depth = material.shape
    angles = angle_orders.shape[0]
    owned = angles // size_x
    group = size_x * size_y
    f32 = jnp.float32
    vmem = functools.partial(pl.BlockSpec, memory_space=pltpu.VMEM)
    smem = functools.partial(pl.BlockSpec, memory_space=pltpu.SMEM)
    hbm = functools.partial(pl.BlockSpec, memory_space=pltpu.HBM)
    dma = pltpu.SemaphoreType.DMA
    planes = pltpu.VMEM((ITERS, 2, cells_y, depth), f32)
    rows = pltpu.VMEM((ITERS, 2, cells_x, 1, depth), f32)
    corner = pltpu.VMEM((ITERS, 8, depth), f32)
    elec, magn, far = pl.pallas_call(
        functools.partial(kernel, size_x, size_y),
        out_shape=(
            jax.ShapeDtypeStruct(e_field.shape, f32),
            jax.ShapeDtypeStruct(h_field.shape, f32),
            jax.ShapeDtypeStruct((4, owned), f32),
        ),
        in_specs=[smem(), smem(), vmem(), hbm(), hbm(), hbm()],
        out_specs=(pl.BlockSpec(memory_space=pl.ANY), pl.BlockSpec(memory_space=pl.ANY), vmem()),
        scratch_shapes=[
            pltpu.VMEM((3, cells_x, cells_y + PAD, depth), f32),
            pltpu.VMEM((3, cells_x, cells_y + PAD, depth), f32),
            pltpu.VMEM((cells_x, cells_y, depth), jnp.int32),
            pltpu.VMEM((2, cells_x, cells_y, depth), f32),
            pltpu.VMEM((cells_y, depth), f32),
            pltpu.VMEM((cells_y, 2 * angles), f32),
            pltpu.VMEM((2 * cells_x, 2 * angles), f32),
            planes, planes, planes, planes,
            rows, rows, rows, rows,
            corner, corner, corner, corner,
            pltpu.VMEM((8, 2 * angles), f32),
            pltpu.VMEM((group, 8, 2 * angles), f32),
            dma((9,)), dma((5,)), dma((ITERS, 6)), dma((ITERS, 6)), dma((group,)), dma((group,)),
        ],
        compiler_params=pltpu.CompilerParams(
            collective_id=0, has_side_effects=True, vmem_limit_bytes=60 * 1024 * 1024
        ),
    )(eps_table, sigma_table, angle_orders.T, e_field, h_field, material)
    return elec, magn, far.T


def solution(mesh):
    return jax.shard_map(
        functools.partial(local, mesh.shape["gx"], mesh.shape["gy"]),
        mesh=mesh,
        in_specs=(
            P(None, ("clip", "gx"), "gy", None),
            P(None, ("clip", "gx"), "gy", None),
            P(("clip", "gx"), "gy", None),
            P(),
            P(),
            P(),
        ),
        out_specs=(
            P(None, ("clip", "gx"), "gy", None),
            P(None, ("clip", "gx"), "gy", None),
            P(("clip", "gx"), None),
        ),
        check_vma=False,
    )
```

```python
import functools
import math

import jax
import jax.numpy as jnp
from jax import lax
from jax.experimental import pallas as pl
from jax.experimental.pallas import tpu as pltpu
from jax.sharding import PartitionSpec as P

ITERS = 4
TIME_STEP = 0.5
PHASE_STEP = 0.9
MESH = pl.DeviceIdType.MESH
PAD = 8
HIGH = lax.Precision.HIGHEST

FWD, BACK, ROW_E, ROW_H, CORNER_E, CORNER_H = 0, 3, 6, 7, 8, 9


def split(low, high):
    return [(r, min(32, high - r)) for r in range(low, high, 32)]


def edge_pieces(cells_y):
    big, mid, small = 3 * cells_y // 4, 5 * cells_y // 8, cells_y // 2
    first = ((0, big), (0, mid), (8, mid), (8, small))
    return [((low, high), (high, cells_y)) + (((0, low),) if low else ()) for low, high in first]


def kernel(
    size_x, size_y,
    eps_ref, sigma_ref, orders_ref, e_in, h_in, mat_in,
    e_out, h_out, far_ref,
    elec, magn, mat, coef, mon, table_y, table_x,
    fwd_send, fwd_recv, back_send, back_recv,
    rowe_send, rowe_recv, rowh_send, rowh_recv,
    core_send, core_recv, corh_send, corh_recv,
    terms_send, terms_recv,
    load_sem, store_sem, send_sem, recv_sem, far_send_sem, far_recv_sem,
):
    cells_x, cells_y, depth = mat.shape
    last = cells_x - 1
    chunk = min(32, cells_y)
    starts = [(r, chunk) for r in range(0, cells_y, chunk)]
    pieces = edge_pieces(cells_y)
    me_x = lax.axis_index("gx")
    me_y = lax.axis_index("gy")
    right = lax.rem(me_x + 1, size_x)
    left = lax.rem(me_x + size_x - 1, size_x)
    above = lax.rem(me_y + 1, size_y)
    below = lax.rem(me_y + size_y - 1, size_y)
    group = size_x * size_y
    me = me_x * size_y + me_y

    def load(src, dst, sem):
        copy = pltpu.make_async_copy(src, dst, load_sem.at[sem])
        copy.start()
        return copy

    inner = pl.ds(0, last)
    ebody = pl.ds(0, cells_y)
    hbody = pl.ds(PAD, cells_y)
    edge_e = load(e_in.at[:, last], elec.at[:, last, ebody], 0)
    edge_h = load(h_in.at[:, last], magn.at[:, last, hbody], 1)
    rest_e = [load(e_in.at[c, inner], elec.at[c, inner, ebody], 2 + c) for c in range(3)]
    rest_h = [load(h_in.at[c, inner], magn.at[c, inner, hbody], 5 + c) for c in range(3)]
    load_mat = load(mat_in, mat, 8)

    def member(offset):
        index = lax.rem(me + offset, group)
        return index // size_y, lax.rem(index, size_y)

    barrier = pltpu.get_barrier_semaphore()
    for offset in range(1, group):
        tx, ty = member(offset)
        pl.semaphore_signal(barrier, inc=1, device_id={"gx": tx, "gy": ty}, device_id_type=MESH)

    def lanes(size):
        return lax.broadcasted_iota(jnp.int32, (size, depth), 1)

    def forward_z(value):
        return jnp.where(lanes(value.shape[0]) == depth - 1, 0.0, pltpu.roll(value, depth - 1, 1)) - value

    def backward_z(value):
        return value - jnp.where(lanes(value.shape[0]) == 0, 0.0, pltpu.roll(value, 1, 1))

    elec[:, :, pl.ds(cells_y, PAD), :] = jnp.zeros((3, cells_x, PAD, depth), jnp.float32)

    def copy_to(phase, kind, src, dst, tx, ty):
        return pltpu.make_async_remote_copy(
            src_ref=src, dst_ref=dst,
            send_sem=send_sem.at[phase, kind], recv_sem=recv_sem.at[phase, kind],
            device_id={"gx": tx, "gy": ty}, device_id_type=MESH,
        )

    def piece_rows(k, piece):
        low, high = pieces[k][piece]
        return pl.ds(low, high - low)

    def fwd_copy(k, piece):
        rows = piece_rows(k, piece)
        return copy_to(k, FWD + piece, fwd_send.at[k, :, rows], fwd_recv.at[k, :, rows], right, me_y)

    def back_copy(k, piece):
        rows = piece_rows(max(k - 1, 0), piece)
        src = e_in.at[pl.ds(1, 2), 0, rows] if k == 0 else back_send.at[k, :, rows]
        return copy_to(k, BACK + piece, src, back_recv.at[k, :, rows], left, me_y)

    def rowe_copy(k):
        return copy_to(k, ROW_E, rowe_send.at[k], rowe_recv.at[k], me_x, below)

    def rowh_copy(k):
        return copy_to(k, ROW_H, rowh_send.at[k], rowh_recv.at[k], me_x, above)

    def core_copy(k):
        return copy_to(k, CORNER_E, core_send.at[k], core_recv.at[k], right, below)

    def corh_copy(k):
        return copy_to(k, CORNER_H, corh_send.at[k], corh_recv.at[k], left, above)

    def magn_plane(x, ahead, stage=None, parts=starts):
        for r, size in parts:
            rows, upper, hrows = pl.ds(r, size), pl.ds(r + 1, size), pl.ds(PAD + r, size)
            ex, ey, ez = elec[0, x, rows], elec[1, x, rows], elec[2, x, rows]
            dyx = elec[0, x, upper] - ex
            dyz = elec[2, x, upper] - ez
            if ahead is None:
                dxy, dxz = -ey, -ez
            else:
                dxy, dxz = elec[1, ahead, rows] - ey, elec[2, ahead, rows] - ez
            hy = magn[1, x, hrows] - TIME_STEP * (forward_z(ex) - dxz)
            hz = magn[2, x, hrows] - TIME_STEP * (dxy - dyx)
            magn[0, x, hrows] = magn[0, x, hrows] - TIME_STEP * (dyz - forward_z(ey))
            magn[1, x, hrows] = hy
            magn[2, x, hrows] = hz
            if stage is not None:
                fwd_send[stage, 0, rows] = hy
                fwd_send[stage, 1, rows] = hz

    def elec_plane(x, previous, number, stage=None, parts=starts):
        cos_n = math.cos(PHASE_STEP * number)
        sin_n = math.sin(PHASE_STEP * number)
        for r, size in parts:
            rows, hrows, lower = pl.ds(r, size), pl.ds(PAD + r, size), pl.ds(PAD + r - 1, size)
            lane = lanes(size)
            hx, hy, hz = magn[0, x, hrows], magn[1, x, hrows], magn[2, x, hrows]
            ex, ey, ez = elec[0, x, rows], elec[1, x, rows], elec[2, x, rows]
            prev_y, prev_z = previous(r, size, ey, ez)
            keep, drive = coef[0, x, rows], coef[1, x, rows]
            new_x = keep * ex + drive * ((hz - magn[2, x, lower]) - backward_z(hy))
            new_y = keep * ey + drive * (backward_z(hx) - (hz - prev_z))
            new_z = keep * ez + drive * ((hy - prev_y) - (hx - magn[0, x, lower]))
            elec[0, x, rows] = new_x
            elec[1, x, rows] = new_y
            elec[2, x, rows] = new_z
            if stage is not None:
                back_send[stage, 0, rows] = new_y
                back_send[stage, 1, rows] = new_z
            total = mon[rows]
            for comp, new in ((0, new_x), (1, new_y)):
                slot = comp * cells_x + x
                weight = jnp.where(lane == slot, cos_n, jnp.where(lane == slot + 2 * cells_x, -sin_n, 0.0))
                total = total + jnp.broadcast_to(new[:, depth - 3:depth - 2], (size, depth)) * weight
            mon[rows] = total

    def local_previous(x):
        def previous(r, size, ey, ez):
            hrows = pl.ds(PAD + r, size)
            return magn[1, x - 1, hrows], magn[2, x - 1, hrows]
        return previous

    def send_corner_h(k):
        corh_send[k] = elec[1, 0, pl.ds(cells_y - 8, 8)]
        corh_copy(k).start()

    def send_corner_e(k):
        core_send[k] = elec[0, last, pl.ds(0, 8)]
        core_copy(k).start()

    mon[...] = jnp.zeros_like(mon)
    terms_send[...] = jnp.zeros_like(terms_send)
    edge_e.wait()
    edge_h.wait()
    magn_plane(last, None, 0)
    pl.semaphore_wait(barrier, group - 1)
    for piece in range(len(pieces[0])):
        back_copy(0, piece).start()
        fwd_copy(0, piece).start()
    send_corner_e(0)
    for copy in rest_e:
        copy.wait()
    send_corner_h(0)
    for copy in rest_h:
        copy.wait()

    row63 = pl.ds(PAD + cells_y - 1, 1)
    halo = pl.ds(PAD - 1, 1)
    row0 = pl.ds(0, 1)

    stores = []

    def store(src, dst):
        copy = pltpu.make_async_copy(src, dst, store_sem.at[len(stores)])
        copy.start()
        stores.append(copy)

    for k in range(ITERS):
        rowe_send[k, 0] = elec[0, :, row0]
        rowe_send[k, 1] = elec[2, :, row0]
        rowe_copy(k).start()
        for x in range(last):
            magn_plane(x, x + 1, parts=starts[-1:])
        rowh_send[k, 0] = magn[0, :, row63]
        rowh_send[k, 1] = magn[2, :, row63]
        rowh_copy(k).start()
        for x in range(last):
            magn_plane(x, x + 1, parts=starts[:-1])
        if k == 0:
            load_mat.wait()
            count = eps_ref.shape[0]
            keeps, drives = [], []
            for m in range(count):
                permit = jnp.full((8, depth), eps_ref[m], jnp.float32)
                conduct = jnp.full((8, depth), sigma_ref[m], jnp.float32)
                loss = conduct * TIME_STEP / (2.0 * permit)
                keeps.append(((1.0 - loss) / (1.0 + loss))[:1])
                drives.append((TIME_STEP / (permit * (1.0 + loss)))[:1])

            def coef_body(x, carry):
                for r, _ in starts:
                    rows = pl.ds(r, chunk)
                    ids = mat[x, rows]
                    keep = jnp.broadcast_to(keeps[0], (chunk, depth))
                    drive = jnp.broadcast_to(drives[0], (chunk, depth))
                    for m in range(1, count):
                        keep = jnp.where(ids == m, keeps[m], keep)
                        drive = jnp.where(ids == m, drives[m], drive)
                    coef[0, x, rows] = keep
                    coef[1, x, rows] = drive
                return carry

            lax.fori_loop(0, cells_x, coef_body, 0)
        if k == 1:
            orders = jnp.concatenate([orders_ref[...], orders_ref[...]], axis=1)
            for table, axis, extent in ((table_y, 1, size_y * cells_y), (table_x, 0, size_x * cells_x)):
                shape = table.shape
                pos = lax.broadcasted_iota(jnp.int32, shape, 0)
                if axis == 1:
                    pos = me_y * cells_y + pos
                else:
                    pos = me_x * cells_x + lax.rem(pos, cells_x)
                turns = (jnp.broadcast_to(orders[axis:axis + 1], shape) * pos).astype(jnp.float32) * (1.0 / extent)
                angle = (turns - jnp.floor(turns)) * (2.0 * math.pi)
                wide = lax.broadcasted_iota(jnp.int32, shape, 1)
                table[...] = jnp.where(wide < shape[1] // 2, jnp.cos(angle), jnp.sin(angle))

        rowe_copy(k).wait_recv()
        rowh_copy(k).wait_recv()
        magn[0, :, row63] = magn[0, :, row63] - TIME_STEP * rowe_recv[k, 1]
        magn[2, :, row63] = magn[2, :, row63] + TIME_STEP * rowe_recv[k, 0]
        magn[0, :, halo] = rowh_recv[k, 0] - TIME_STEP * elec[2, :, row0]
        magn[2, :, halo] = rowh_recv[k, 1] + TIME_STEP * elec[0, :, row0]

        for x in range(1, last):
            elec_plane(x, local_previous(x), k + 1)
        final = k == ITERS - 1
        if final:
            store(magn.at[:, inner, hbody], h_out.at[:, inner])
            store(elec.at[:, pl.ds(1, last - 1), ebody], e_out.at[:, pl.ds(1, last - 1)])

        def received(r, size, ey, ez):
            rows = pl.ds(r, size)
            return fwd_recv[k, 0, rows] + TIME_STEP * ez, fwd_recv[k, 1, rows] - TIME_STEP * ey

        def first_plane(piece):
            for at in ((0,) if piece == 0 else range(1, len(pieces[k]))):
                fwd_copy(k, at).wait_recv()
            if piece == 1:
                core_copy(k).wait_recv()
                fwd_recv[k, 1, pl.ds(cells_y - 1, 1)] = (
                    fwd_recv[k, 1, pl.ds(cells_y - 1, 1)] + TIME_STEP * core_recv[k, pl.ds(0, 1)]
                )
            for at in ((0,) if piece == 0 else range(1, len(pieces[k]))):
                elec_plane(0, received, k + 1, None if final else k + 1, split(*pieces[k][at]))
                if not final:
                    back_copy(k + 1, at).start()
            if piece == 1 and not final:
                send_corner_h(k + 1)

        back_pieces = pieces[max(k - 1, 0)]

        def add_ahead(low, high):
            for r, size in split(low, high):
                rows, hrows = pl.ds(r, size), pl.ds(PAD + r, size)
                magn[1, last, hrows] = magn[1, last, hrows] + TIME_STEP * back_recv[k, 1, rows]
                magn[2, last, hrows] = magn[2, last, hrows] - TIME_STEP * back_recv[k, 0, rows]

        def last_halo():
            corh_copy(k).wait_recv()
            magn[2, last, halo] = magn[2, last, halo] - TIME_STEP * corh_recv[k, pl.ds(7, 1)]

        def last_elec(low, high):
            elec_plane(last, local_previous(last), k + 1, None, split(low, high))

        def last_magn(low, high):
            magn_plane(last, None, k + 1, split(low, high))

        early_high = back_pieces[0][1]
        early_low = back_pieces[0][0] + 8 if final else pieces[k + 1][0][0]

        first_plane(0)
        back_copy(k, 0).wait_recv()
        add_ahead(*back_pieces[0])
        if k == 0:
            last_halo()
        last_elec(early_low, early_high)
        if not final:
            low, high = pieces[k + 1][0]
            last_magn(low, high)
            fwd_copy(k + 1, 0).start()
        first_plane(1)
        if final:
            store(elec.at[:, 0, ebody], e_out.at[:, 0])
        for at in range(1, len(back_pieces)):
            back_copy(k, at).wait_recv()
            add_ahead(*back_pieces[at])
        if k > 0:
            last_halo()
        if early_low:
            last_elec(0, early_low)
        last_elec(early_high, cells_y)
        if not final:
            for at in range(1, len(pieces[k + 1])):
                last_magn(*pieces[k + 1][at])
                fwd_copy(k + 1, at).start()
            send_corner_e(k + 1)
        else:
            store(magn.at[:, last, hbody], h_out.at[:, last])
            store(elec.at[:, last, ebody], e_out.at[:, last])

    span = 2 * cells_x
    total = jnp.transpose(mon[...])[:2 * span]
    by_cos = jnp.dot(total, table_y[...], precision=HIGH, preferred_element_type=jnp.float32)
    angles = by_cos.shape[1] // 2
    by_sin = pltpu.roll(by_cos, angles, 1)
    part_re = by_cos[:span] + by_sin[span:]
    part_im = by_cos[span:] - by_sin[:span]
    cos_x = table_x[...]
    sin_x = pltpu.roll(cos_x, angles, 1)
    real = cos_x * part_re + sin_x * part_im
    imag = cos_x * part_im - sin_x * part_re
    for row, value in enumerate((real[:cells_x], imag[:cells_x], real[cells_x:], imag[cells_x:])):
        terms_send[row:row + 1] = jnp.sum(value, axis=0, keepdims=True)

    def far_copy(offset):
        tx, ty = member(offset)
        return pltpu.make_async_remote_copy(
            src_ref=terms_send, dst_ref=terms_recv.at[me],
            send_sem=far_send_sem.at[offset], recv_sem=far_recv_sem.at[me],
            device_id={"gx": tx, "gy": ty}, device_id_type=MESH,
        )

    for offset in range(1, group):
        far_copy(offset).start()
    answer = terms_send[...]
    for offset in range(1, group):
        source = lax.rem(me + offset, group)
        pltpu.make_async_remote_copy(
            src_ref=terms_send, dst_ref=terms_recv.at[source],
            send_sem=far_send_sem.at[offset], recv_sem=far_recv_sem.at[source],
            device_id={"gx": right, "gy": me_y}, device_id_type=MESH,
        ).wait_recv()
        answer = answer + terms_recv[source]
    owned = far_ref.shape[1]
    width = answer.shape[1]
    mine = pltpu.roll(answer, lax.rem(width - owned * me_x, width), 1)
    scale = 1.0 / math.sqrt(size_x * cells_x * size_y * cells_y)
    far_ref[...] = mine[:4, :owned] * scale

    for copy in stores:
        copy.wait()
    for k in range(ITERS):
        for copy in (rowe_copy, rowh_copy, core_copy, corh_copy):
            copy(k).wait_send()
        for piece in range(len(pieces[k])):
            fwd_copy(k, piece).wait_send()
        for piece in range(len(pieces[max(k - 1, 0)])):
            back_copy(k, piece).wait_send()
    for offset in range(1, group):
        far_copy(offset).wait_send()


def place(e_raw, h_raw, far_raw, e_out, h_out, far_out, e_held, h_held, far_held, in_sem, out_sem):
    pairs = []
    for x in range(0, e_raw.shape[1], 2):
        planes = pl.ds(x, 2)
        for c in range(3):
            for raw, held, out in ((e_raw, e_held, e_out), (h_raw, h_held, h_out)):
                pairs.append((raw.at[c, planes], held.at[c, planes], out.at[c, planes]))
    pairs.append((far_raw, far_held, far_out))
    loads = [pltpu.make_async_copy(raw, held, in_sem.at[i]) for i, (raw, held, _) in enumerate(pairs)]
    saves = [pltpu.make_async_copy(held, out, out_sem.at[i]) for i, (_, held, out) in enumerate(pairs)]
    for copy in loads:
        copy.start()
    for copy, save in zip(loads, saves):
        copy.wait()
        save.start()
    for save in saves:
        save.wait()


def local(size_x, size_y, e_field, h_field, material, eps_table, sigma_table, angle_orders):
    cells_x, cells_y, depth = material.shape
    angles = angle_orders.shape[0]
    owned = angles // size_x
    group = size_x * size_y
    f32 = jnp.float32
    vmem = functools.partial(pl.BlockSpec, memory_space=pltpu.VMEM)
    smem = functools.partial(pl.BlockSpec, memory_space=pltpu.SMEM)
    hbm = functools.partial(pl.BlockSpec, memory_space=pltpu.HBM)
    dma = pltpu.SemaphoreType.DMA
    planes = pltpu.VMEM((ITERS, 2, cells_y, depth), f32)
    rows = pltpu.VMEM((ITERS, 2, cells_x, 1, depth), f32)
    corner = pltpu.VMEM((ITERS, 8, depth), f32)
    elec, magn, far = pl.pallas_call(
        functools.partial(kernel, size_x, size_y),
        out_shape=(
            jax.ShapeDtypeStruct(e_field.shape, f32),
            jax.ShapeDtypeStruct(h_field.shape, f32),
            jax.ShapeDtypeStruct((4, owned), f32),
        ),
        in_specs=[smem(), smem(), vmem(), hbm(), hbm(), hbm()],
        out_specs=(pl.BlockSpec(memory_space=pl.ANY), pl.BlockSpec(memory_space=pl.ANY), vmem()),
        scratch_shapes=[
            pltpu.VMEM((3, cells_x, cells_y + PAD, depth), f32),
            pltpu.VMEM((3, cells_x, cells_y + PAD, depth), f32),
            pltpu.VMEM((cells_x, cells_y, depth), jnp.int32),
            pltpu.VMEM((2, cells_x, cells_y, depth), f32),
            pltpu.VMEM((cells_y, depth), f32),
            pltpu.VMEM((cells_y, 2 * angles), f32),
            pltpu.VMEM((2 * cells_x, 2 * angles), f32),
            planes, planes, planes, planes,
            rows, rows, rows, rows,
            corner, corner, corner, corner,
            pltpu.VMEM((8, 2 * angles), f32),
            pltpu.VMEM((group, 8, 2 * angles), f32),
            dma((9,)), dma((5,)), dma((ITERS, 10)), dma((ITERS, 10)), dma((group,)), dma((group,)),
        ],
        compiler_params=pltpu.CompilerParams(
            collective_id=0, has_side_effects=True, vmem_limit_bytes=60 * 1024 * 1024
        ),
    )(eps_table, sigma_table, angle_orders.T, e_field, h_field, material)
    elec, magn, far = pl.pallas_call(
        place,
        out_shape=tuple(jax.ShapeDtypeStruct(value.shape, f32) for value in (elec, magn, far)),
        in_specs=[hbm()] * 3,
        out_specs=(hbm(),) * 3,
        scratch_shapes=[
            pltpu.VMEM(elec.shape, f32), pltpu.VMEM(magn.shape, f32), pltpu.VMEM(far.shape, f32),
            dma((3 * cells_x + 1,)), dma((3 * cells_x + 1,)),
        ],
        compiler_params=pltpu.CompilerParams(vmem_limit_bytes=60 * 1024 * 1024),
    )(elec, magn, far)
    return elec, magn, far.T


def solution(mesh):
    return jax.shard_map(
        functools.partial(local, mesh.shape["gx"], mesh.shape["gy"]),
        mesh=mesh,
        in_specs=(
            P(None, ("clip", "gx"), "gy", None),
            P(None, ("clip", "gx"), "gy", None),
            P(("clip", "gx"), "gy", None),
            P(),
            P(),
            P(),
        ),
        out_specs=(
            P(None, ("clip", "gx"), "gy", None),
            P(None, ("clip", "gx"), "gy", None),
            P(("clip", "gx"), None),
        ),
        check_vma=False,
    )
```

```python
import functools
import math

import jax
import jax.numpy as jnp
from jax import lax
from jax.experimental import pallas as pl
from jax.experimental.pallas import tpu as pltpu
from jax.sharding import PartitionSpec as P

ITERS = 4
TIME_STEP = 0.5
PHASE_STEP = 0.9
MESH = pl.DeviceIdType.MESH
PAD = 8
HIGH = lax.Precision.HIGHEST

FWD, BACK, ROW_E, ROW_H, CORNER_E, CORNER_H = 0, 3, 6, 7, 8, 9


def split(low, high):
    return [(r, min(32, high - r)) for r in range(low, high, 32)]


def edge_pieces(cells_y):
    big, mid, small = 3 * cells_y // 4, 5 * cells_y // 8, cells_y // 2
    first = ((0, big), (0, mid), (8, mid), (8, small))
    return [((low, high), (high, cells_y)) + (((0, low),) if low else ()) for low, high in first]


def kernel(
    size_x, size_y,
    eps_ref, sigma_ref, orders_ref, e_in, h_in, mat_in,
    e_out, h_out, far_ref,
    elec, magn, mat, coef, mon, table_y, table_x,
    fwd_send, fwd_recv, back_send, back_recv,
    rowe_send, rowe_recv, rowh_send, rowh_recv,
    core_send, core_recv, corh_send, corh_recv,
    terms_send, terms_recv,
    load_sem, store_sem, send_sem, recv_sem, far_send_sem, far_recv_sem,
):
    cells_x, cells_y, depth = mat.shape
    last = cells_x - 1
    chunk = min(32, cells_y)
    starts = [(r, chunk) for r in range(0, cells_y, chunk)]
    pieces = edge_pieces(cells_y)
    me_x = lax.axis_index("gx")
    me_y = lax.axis_index("gy")
    right = lax.rem(me_x + 1, size_x)
    left = lax.rem(me_x + size_x - 1, size_x)
    above = lax.rem(me_y + 1, size_y)
    below = lax.rem(me_y + size_y - 1, size_y)
    group = size_x * size_y
    me = me_x * size_y + me_y

    def load(src, dst, sem):
        copy = pltpu.make_async_copy(src, dst, load_sem.at[sem])
        copy.start()
        return copy

    inner = pl.ds(0, last)
    ebody = pl.ds(0, cells_y)
    hbody = pl.ds(PAD, cells_y)
    edge_e = load(e_in.at[:, last], elec.at[:, last, ebody], 0)
    edge_h = load(h_in.at[:, last], magn.at[:, last, hbody], 1)
    rest_e = [load(e_in.at[c, inner], elec.at[c, inner, ebody], 2 + c) for c in range(3)]
    rest_h = [load(h_in.at[c, inner], magn.at[c, inner, hbody], 5 + c) for c in range(3)]
    load_mat = load(mat_in, mat, 8)

    def member(offset):
        index = lax.rem(me + offset, group)
        return index // size_y, lax.rem(index, size_y)

    barrier = pltpu.get_barrier_semaphore()
    for offset in range(1, group):
        tx, ty = member(offset)
        pl.semaphore_signal(barrier, inc=1, device_id={"gx": tx, "gy": ty}, device_id_type=MESH)

    def lanes(size):
        return lax.broadcasted_iota(jnp.int32, (size, depth), 1)

    def forward_z(value):
        return jnp.where(lanes(value.shape[0]) == depth - 1, 0.0, pltpu.roll(value, depth - 1, 1)) - value

    def backward_z(value):
        return value - jnp.where(lanes(value.shape[0]) == 0, 0.0, pltpu.roll(value, 1, 1))

    elec[:, :, pl.ds(cells_y, PAD), :] = jnp.zeros((3, cells_x, PAD, depth), jnp.float32)

    def copy_to(phase, kind, src, dst, tx, ty):
        return pltpu.make_async_remote_copy(
            src_ref=src, dst_ref=dst,
            send_sem=send_sem.at[phase, kind], recv_sem=recv_sem.at[phase, kind],
            device_id={"gx": tx, "gy": ty}, device_id_type=MESH,
        )

    def piece_rows(k, piece):
        low, high = pieces[k][piece]
        return pl.ds(low, high - low)

    def fwd_copy(k, piece):
        rows = piece_rows(k, piece)
        return copy_to(k, FWD + piece, fwd_send.at[k, :, rows], fwd_recv.at[k, :, rows], right, me_y)

    def back_copy(k, piece):
        rows = piece_rows(max(k - 1, 0), piece)
        src = e_in.at[pl.ds(1, 2), 0, rows] if k == 0 else back_send.at[k, :, rows]
        return copy_to(k, BACK + piece, src, back_recv.at[k, :, rows], left, me_y)

    def rowe_copy(k):
        return copy_to(k, ROW_E, rowe_send.at[k], rowe_recv.at[k], me_x, below)

    def rowh_copy(k):
        return copy_to(k, ROW_H, rowh_send.at[k], rowh_recv.at[k], me_x, above)

    def core_copy(k):
        return copy_to(k, CORNER_E, core_send.at[k], core_recv.at[k], right, below)

    def corh_copy(k):
        return copy_to(k, CORNER_H, corh_send.at[k], corh_recv.at[k], left, above)

    def magn_plane(x, ahead, stage=None, parts=starts):
        for r, size in parts:
            rows, upper, hrows = pl.ds(r, size), pl.ds(r + 1, size), pl.ds(PAD + r, size)
            ex, ey, ez = elec[0, x, rows], elec[1, x, rows], elec[2, x, rows]
            dyx = elec[0, x, upper] - ex
            dyz = elec[2, x, upper] - ez
            if ahead is None:
                dxy, dxz = -ey, -ez
            else:
                dxy, dxz = elec[1, ahead, rows] - ey, elec[2, ahead, rows] - ez
            hy = magn[1, x, hrows] - TIME_STEP * (forward_z(ex) - dxz)
            hz = magn[2, x, hrows] - TIME_STEP * (dxy - dyx)
            magn[0, x, hrows] = magn[0, x, hrows] - TIME_STEP * (dyz - forward_z(ey))
            magn[1, x, hrows] = hy
            magn[2, x, hrows] = hz
            if stage is not None:
                fwd_send[stage, 0, rows] = hy
                fwd_send[stage, 1, rows] = hz

    def elec_plane(x, previous, number, stage=None, parts=starts):
        cos_n = math.cos(PHASE_STEP * number)
        sin_n = math.sin(PHASE_STEP * number)
        for r, size in parts:
            rows, hrows, lower = pl.ds(r, size), pl.ds(PAD + r, size), pl.ds(PAD + r - 1, size)
            lane = lanes(size)
            hx, hy, hz = magn[0, x, hrows], magn[1, x, hrows], magn[2, x, hrows]
            ex, ey, ez = elec[0, x, rows], elec[1, x, rows], elec[2, x, rows]
            prev_y, prev_z = previous(r, size, ey, ez)
            keep, drive = coef[0, x, rows], coef[1, x, rows]
            new_x = keep * ex + drive * ((hz - magn[2, x, lower]) - backward_z(hy))
            new_y = keep * ey + drive * (backward_z(hx) - (hz - prev_z))
            new_z = keep * ez + drive * ((hy - prev_y) - (hx - magn[0, x, lower]))
            elec[0, x, rows] = new_x
            elec[1, x, rows] = new_y
            elec[2, x, rows] = new_z
            if stage is not None:
                back_send[stage, 0, rows] = new_y
                back_send[stage, 1, rows] = new_z
            total = mon[rows]
            for comp, new in ((0, new_x), (1, new_y)):
                slot = comp * cells_x + x
                weight = jnp.where(lane == slot, cos_n, jnp.where(lane == slot + 2 * cells_x, -sin_n, 0.0))
                total = total + jnp.broadcast_to(new[:, depth - 3:depth - 2], (size, depth)) * weight
            mon[rows] = total

    def local_previous(x):
        def previous(r, size, ey, ez):
            hrows = pl.ds(PAD + r, size)
            return magn[1, x - 1, hrows], magn[2, x - 1, hrows]
        return previous

    def send_corner_h(k):
        corh_send[k] = elec[1, 0, pl.ds(cells_y - 8, 8)]
        corh_copy(k).start()

    def send_corner_e(k):
        core_send[k] = elec[0, last, pl.ds(0, 8)]
        core_copy(k).start()

    mon[...] = jnp.zeros_like(mon)
    terms_send[...] = jnp.zeros_like(terms_send)
    edge_e.wait()
    edge_h.wait()
    magn_plane(last, None, 0)
    pl.semaphore_wait(barrier, group - 1)
    for piece in range(len(pieces[0])):
        back_copy(0, piece).start()
        fwd_copy(0, piece).start()
    send_corner_e(0)
    for copy in rest_e:
        copy.wait()
    send_corner_h(0)
    for copy in rest_h:
        copy.wait()

    row63 = pl.ds(PAD + cells_y - 1, 1)
    halo = pl.ds(PAD - 1, 1)
    row0 = pl.ds(0, 1)

    stores = []

    def store(src, dst):
        copy = pltpu.make_async_copy(src, dst, store_sem.at[len(stores)])
        copy.start()
        stores.append(copy)

    for k in range(ITERS):
        rowe_send[k, 0] = elec[0, :, row0]
        rowe_send[k, 1] = elec[2, :, row0]
        rowe_copy(k).start()
        for x in range(last):
            magn_plane(x, x + 1, parts=starts[-1:])
        rowh_send[k, 0] = magn[0, :, row63]
        rowh_send[k, 1] = magn[2, :, row63]
        rowh_copy(k).start()
        for x in range(last):
            magn_plane(x, x + 1, parts=starts[:-1])
        if k == 0:
            load_mat.wait()
            count = eps_ref.shape[0]
            keeps, drives = [], []
            for m in range(count):
                permit = jnp.full((8, depth), eps_ref[m], jnp.float32)
                conduct = jnp.full((8, depth), sigma_ref[m], jnp.float32)
                loss = conduct * TIME_STEP / (2.0 * permit)
                keeps.append(((1.0 - loss) / (1.0 + loss))[:1])
                drives.append((TIME_STEP / (permit * (1.0 + loss)))[:1])

            def coef_body(x, carry):
                for r, _ in starts:
                    rows = pl.ds(r, chunk)
                    ids = mat[x, rows]
                    keep = jnp.broadcast_to(keeps[0], (chunk, depth))
                    drive = jnp.broadcast_to(drives[0], (chunk, depth))
                    for m in range(1, count):
                        keep = jnp.where(ids == m, keeps[m], keep)
                        drive = jnp.where(ids == m, drives[m], drive)
                    coef[0, x, rows] = keep
                    coef[1, x, rows] = drive
                return carry

            lax.fori_loop(0, cells_x, coef_body, 0)
        if k == 1:
            orders = jnp.concatenate([orders_ref[...], orders_ref[...]], axis=1)
            for table, axis, extent in ((table_y, 1, size_y * cells_y), (table_x, 0, size_x * cells_x)):
                shape = table.shape
                pos = lax.broadcasted_iota(jnp.int32, shape, 0)
                if axis == 1:
                    pos = me_y * cells_y + pos
                else:
                    pos = me_x * cells_x + lax.rem(pos, cells_x)
                turns = (jnp.broadcast_to(orders[axis:axis + 1], shape) * pos).astype(jnp.float32) * (1.0 / extent)
                angle = (turns - jnp.floor(turns)) * (2.0 * math.pi)
                wide = lax.broadcasted_iota(jnp.int32, shape, 1)
                table[...] = jnp.where(wide < shape[1] // 2, jnp.cos(angle), jnp.sin(angle))

        rowe_copy(k).wait_recv()
        rowh_copy(k).wait_recv()
        magn[0, :, row63] = magn[0, :, row63] - TIME_STEP * rowe_recv[k, 1]
        magn[2, :, row63] = magn[2, :, row63] + TIME_STEP * rowe_recv[k, 0]
        magn[0, :, halo] = rowh_recv[k, 0] - TIME_STEP * elec[2, :, row0]
        magn[2, :, halo] = rowh_recv[k, 1] + TIME_STEP * elec[0, :, row0]

        for x in range(1, last):
            elec_plane(x, local_previous(x), k + 1)
        final = k == ITERS - 1
        if final:
            store(magn.at[:, inner, hbody], h_out.at[:, inner])
            store(elec.at[:, pl.ds(1, last - 1), ebody], e_out.at[:, pl.ds(1, last - 1)])

        def received(r, size, ey, ez):
            rows = pl.ds(r, size)
            return fwd_recv[k, 0, rows] + TIME_STEP * ez, fwd_recv[k, 1, rows] - TIME_STEP * ey

        def first_plane(piece):
            for at in ((0,) if piece == 0 else range(1, len(pieces[k]))):
                fwd_copy(k, at).wait_recv()
            if piece == 1:
                core_copy(k).wait_recv()
                fwd_recv[k, 1, pl.ds(cells_y - 1, 1)] = (
                    fwd_recv[k, 1, pl.ds(cells_y - 1, 1)] + TIME_STEP * core_recv[k, pl.ds(0, 1)]
                )
            for at in ((0,) if piece == 0 else range(1, len(pieces[k]))):
                elec_plane(0, received, k + 1, None if final else k + 1, split(*pieces[k][at]))
                if not final:
                    back_copy(k + 1, at).start()
            if piece == 1 and not final:
                send_corner_h(k + 1)

        back_pieces = pieces[max(k - 1, 0)]

        def add_ahead(low, high):
            for r, size in split(low, high):
                rows, hrows = pl.ds(r, size), pl.ds(PAD + r, size)
                magn[1, last, hrows] = magn[1, last, hrows] + TIME_STEP * back_recv[k, 1, rows]
                magn[2, last, hrows] = magn[2, last, hrows] - TIME_STEP * back_recv[k, 0, rows]

        def last_halo():
            corh_copy(k).wait_recv()
            magn[2, last, halo] = magn[2, last, halo] - TIME_STEP * corh_recv[k, pl.ds(7, 1)]

        def last_elec(low, high):
            elec_plane(last, local_previous(last), k + 1, None, split(low, high))

        def last_magn(low, high):
            magn_plane(last, None, k + 1, split(low, high))

        early_high = back_pieces[0][1]
        early_low = back_pieces[0][0] + 8 if final else pieces[k + 1][0][0]

        first_plane(0)
        back_copy(k, 0).wait_recv()
        add_ahead(*back_pieces[0])
        if k == 0:
            last_halo()
        last_elec(early_low, early_high)
        if not final:
            low, high = pieces[k + 1][0]
            last_magn(low, high)
            fwd_copy(k + 1, 0).start()
        first_plane(1)
        if final:
            store(elec.at[:, 0, ebody], e_out.at[:, 0])
        for at in range(1, len(back_pieces)):
            back_copy(k, at).wait_recv()
            add_ahead(*back_pieces[at])
        if k > 0:
            last_halo()
        if early_low:
            last_elec(0, early_low)
        last_elec(early_high, cells_y)
        if not final:
            for at in range(1, len(pieces[k + 1])):
                last_magn(*pieces[k + 1][at])
                fwd_copy(k + 1, at).start()
            send_corner_e(k + 1)
        else:
            store(magn.at[:, last, hbody], h_out.at[:, last])
            store(elec.at[:, last, ebody], e_out.at[:, last])

    span = 2 * cells_x
    total = jnp.transpose(mon[...])[:2 * span]
    by_cos = jnp.dot(total, table_y[...], precision=HIGH, preferred_element_type=jnp.float32)
    angles = by_cos.shape[1] // 2
    by_sin = pltpu.roll(by_cos, angles, 1)
    part_re = by_cos[:span] + by_sin[span:]
    part_im = by_cos[span:] - by_sin[:span]
    cos_x = table_x[...]
    sin_x = pltpu.roll(cos_x, angles, 1)
    real = cos_x * part_re + sin_x * part_im
    imag = cos_x * part_im - sin_x * part_re
    for row, value in enumerate((real[:cells_x], imag[:cells_x], real[cells_x:], imag[cells_x:])):
        terms_send[row:row + 1] = jnp.sum(value, axis=0, keepdims=True)

    def far_copy(offset):
        tx, ty = member(offset)
        return pltpu.make_async_remote_copy(
            src_ref=terms_send, dst_ref=terms_recv.at[me],
            send_sem=far_send_sem.at[offset], recv_sem=far_recv_sem.at[me],
            device_id={"gx": tx, "gy": ty}, device_id_type=MESH,
        )

    for offset in range(1, group):
        far_copy(offset).start()
    answer = terms_send[...]
    for offset in range(1, group):
        source = lax.rem(me + offset, group)
        pltpu.make_async_remote_copy(
            src_ref=terms_send, dst_ref=terms_recv.at[source],
            send_sem=far_send_sem.at[offset], recv_sem=far_recv_sem.at[source],
            device_id={"gx": right, "gy": me_y}, device_id_type=MESH,
        ).wait_recv()
        answer = answer + terms_recv[source]
    owned = far_ref.shape[1]
    width = answer.shape[1]
    mine = pltpu.roll(answer, lax.rem(width - owned * me_x, width), 1)
    scale = 1.0 / math.sqrt(size_x * cells_x * size_y * cells_y)
    far_ref[...] = mine[:4, :owned] * scale

    for copy in stores:
        copy.wait()
    for k in range(ITERS):
        for copy in (rowe_copy, rowh_copy, core_copy, corh_copy):
            copy(k).wait_send()
        for piece in range(len(pieces[k])):
            fwd_copy(k, piece).wait_send()
        for piece in range(len(pieces[max(k - 1, 0)])):
            back_copy(k, piece).wait_send()
    for offset in range(1, group):
        far_copy(offset).wait_send()


def place(e_raw, h_raw, far_raw, e_out, h_out, far_out, e_held, h_held, far_held, in_sem, out_sem):
    pairs = []
    for c in range(e_raw.shape[0]):
        for raw, held, out in ((e_raw, e_held, e_out), (h_raw, h_held, h_out)):
            pairs.append((raw.at[c], held.at[c], out.at[c]))
    pairs.append((far_raw, far_held, far_out))
    loads = [pltpu.make_async_copy(raw, held, in_sem.at[i]) for i, (raw, held, _) in enumerate(pairs)]
    saves = [pltpu.make_async_copy(held, out, out_sem.at[i]) for i, (_, held, out) in enumerate(pairs)]
    for copy in loads:
        copy.start()
    for copy, save in zip(loads, saves):
        copy.wait()
        save.start()
    for save in saves:
        save.wait()


def local(size_x, size_y, e_field, h_field, material, eps_table, sigma_table, angle_orders):
    cells_x, cells_y, depth = material.shape
    angles = angle_orders.shape[0]
    owned = angles // size_x
    group = size_x * size_y
    f32 = jnp.float32
    vmem = functools.partial(pl.BlockSpec, memory_space=pltpu.VMEM)
    smem = functools.partial(pl.BlockSpec, memory_space=pltpu.SMEM)
    hbm = functools.partial(pl.BlockSpec, memory_space=pltpu.HBM)
    dma = pltpu.SemaphoreType.DMA
    planes = pltpu.VMEM((ITERS, 2, cells_y, depth), f32)
    rows = pltpu.VMEM((ITERS, 2, cells_x, 1, depth), f32)
    corner = pltpu.VMEM((ITERS, 8, depth), f32)
    elec, magn, far = pl.pallas_call(
        functools.partial(kernel, size_x, size_y),
        out_shape=(
            jax.ShapeDtypeStruct(e_field.shape, f32),
            jax.ShapeDtypeStruct(h_field.shape, f32),
            jax.ShapeDtypeStruct((4, owned), f32),
        ),
        in_specs=[smem(), smem(), vmem(), hbm(), hbm(), hbm()],
        out_specs=(pl.BlockSpec(memory_space=pl.ANY), pl.BlockSpec(memory_space=pl.ANY), vmem()),
        scratch_shapes=[
            pltpu.VMEM((3, cells_x, cells_y + PAD, depth), f32),
            pltpu.VMEM((3, cells_x, cells_y + PAD, depth), f32),
            pltpu.VMEM((cells_x, cells_y, depth), jnp.int32),
            pltpu.VMEM((2, cells_x, cells_y, depth), f32),
            pltpu.VMEM((cells_y, depth), f32),
            pltpu.VMEM((cells_y, 2 * angles), f32),
            pltpu.VMEM((2 * cells_x, 2 * angles), f32),
            planes, planes, planes, planes,
            rows, rows, rows, rows,
            corner, corner, corner, corner,
            pltpu.VMEM((8, 2 * angles), f32),
            pltpu.VMEM((group, 8, 2 * angles), f32),
            dma((9,)), dma((5,)), dma((ITERS, 10)), dma((ITERS, 10)), dma((group,)), dma((group,)),
        ],
        compiler_params=pltpu.CompilerParams(
            collective_id=0, has_side_effects=True, vmem_limit_bytes=60 * 1024 * 1024
        ),
    )(eps_table, sigma_table, angle_orders.T, e_field, h_field, material)
    elec, magn, far = pl.pallas_call(
        place,
        out_shape=tuple(jax.ShapeDtypeStruct(value.shape, f32) for value in (elec, magn, far)),
        in_specs=[hbm()] * 3,
        out_specs=(hbm(),) * 3,
        scratch_shapes=[
            pltpu.VMEM(elec.shape, f32), pltpu.VMEM(magn.shape, f32), pltpu.VMEM(far.shape, f32),
            dma((7,)), dma((7,)),
        ],
        compiler_params=pltpu.CompilerParams(vmem_limit_bytes=60 * 1024 * 1024),
    )(elec, magn, far)
    return elec, magn, far.T


def solution(mesh):
    return jax.shard_map(
        functools.partial(local, mesh.shape["gx"], mesh.shape["gy"]),
        mesh=mesh,
        in_specs=(
            P(None, ("clip", "gx"), "gy", None),
            P(None, ("clip", "gx"), "gy", None),
            P(("clip", "gx"), "gy", None),
            P(),
            P(),
            P(),
        ),
        out_specs=(
            P(None, ("clip", "gx"), "gy", None),
            P(None, ("clip", "gx"), "gy", None),
            P(("clip", "gx"), None),
        ),
        check_vma=False,
    )
```
